32 devices in a mesh: group: 4 (over z), dev: 8 (over y, x, core).
Axes of the slice: x: 2, y: 2, z: 4, core: 2. Of those that a mesh axis runs over, the one named last changes fastest.
Arguments:
- start: float32 [512, 256], P(('group', 'dev')), may hold values from -12 to 12
- coords: float32 [512, 3, 256], P(('group', 'dev')), may hold values from -1 to 1
- area: float32 [512, 256], P(('group', 'dev')), may hold values from 0.1 to 0.4
- near_list: int32 [512, 6], P(('group', 'dev')), may hold values from -1 to 511, as said below
- basis: float32 [512, 64, 256], P(('group', 'dev')), may hold values from -0.375 to 0.375
- far_leaf: int32 [512, 8], P(('group', 'dev')), may hold values from 0 to 127
- couple_leaf: float32 [512, 64, 512], P(('group', 'dev')), may hold values from -0.25 to 0.25
- transfer: float32 [32, 64, 1024], P(('group', 'dev')), may hold values from -0.375 to 0.375
- far_top: int32 [32, 16], P(('group', 'dev')), may hold values from 0 to 31
- couple_top: float32 [32, 64, 1024], P(('group', 'dev')), may hold values from -0.1875 to 0.1875
Outputs:
- product_first: float32 [512, 256], P(('group', 'dev'))
- product_second: float32 [512, 256], P(('group', 'dev'))
The draws below stay inside these ranges and needn't reach their ends.
Inputs may be any that keep to these rules, and one draw needn't show every extreme that they name: `near_list`: row i names leaf i once and otherwise leaves of the same group, none twice; -1 marks an unused entry. Over the rows of one device, the named leaves that lie on other devices come from exactly 4 devices, exactly 8 distinct leaves from each.
All inputs are finite; a program needn't handle non-finite values.
Results may differ from the reference program's by a relative error of at most 0.0003.
Values sent between devices are 32-bit elements; how exact they have to be, the bound alone decides.
A program may use at most 64 MiB of HBM per device.

```python
import math
import jax
import jax.numpy as jnp
from jax import lax

LEAF = 256
RANK = 64
L_DEV = 16
NEAR = 6
NREMOTE = 2
FAR = 8
FAR_TOP = 16
CAP = 8
NLEAF = 512
PANELS = 131072
N_DEV = 8
DEVICES = 32


def draw_start(key, part):
    key = jax.random.fold_in(key, 5)
    first_key = jax.random.fold_in(key, 0)
    rising = 1.0 + 2.0 * jnp.arange(NLEAF, dtype=jnp.float32) / NLEAF
    values = jnp.clip(jax.random.normal(first_key, (NLEAF, LEAF), jnp.float32), -4.0, 4.0)
    return (values * rising[:, None]).astype(jnp.float32)


def draw_near_list(key, part):
    key = jax.random.fold_in(key, 17)
    key_peers, key_leaves, key_offsets, key_drops, key_order = jax.random.split(key, 5)
    peer_count = N_DEV // 2
    local_count = NEAR - 1 - NREMOTE
    device_ids = jnp.arange(DEVICES, dtype=jnp.int32)
    within = device_ids % N_DEV
    group_base = device_ids // N_DEV * N_DEV

    def pick_peers(single_key):
        return jax.random.permutation(single_key, N_DEV - 1)[:peer_count].astype(jnp.int32)
    peer_rel = jax.vmap(pick_peers)(jax.random.split(key_peers, DEVICES))
    peer_device = group_base[:, None] + (within[:, None] + 1 + peer_rel) % N_DEV

    def pick_leaves(single_key):
        return jax.random.permutation(single_key, L_DEV)[:CAP].astype(jnp.int32)
    leaf_pick = jax.vmap(pick_leaves)(jax.random.split(key_leaves, DEVICES * peer_count))
    leaf_pick = leaf_pick.reshape(DEVICES, peer_count, CAP)
    entry = jnp.arange(L_DEV * NREMOTE, dtype=jnp.int32)
    peer_slot = entry % peer_count
    leaf_slot = entry // peer_count
    remote = peer_device[:, peer_slot] * L_DEV + leaf_pick[:, peer_slot, leaf_slot]
    remote = remote.reshape(DEVICES, L_DEV, NREMOTE)

    def pick_offsets(single_key):
        return 1 + jax.random.permutation(single_key, L_DEV - 1)[:local_count].astype(jnp.int32)
    offsets = jax.vmap(pick_offsets)(jax.random.split(key_offsets, DEVICES * L_DEV))
    offsets = offsets.reshape(DEVICES, L_DEV, local_count)
    leaf_index = jnp.arange(L_DEV, dtype=jnp.int32)
    nearby = device_ids[:, None, None] * L_DEV + (leaf_index[None, :, None] + offsets) % L_DEV
    dropped = jax.random.randint(key_drops, (DEVICES, L_DEV, local_count), 0, 3) == 0
    nearby = jnp.where(dropped, -1, nearby)
    itself = (device_ids[:, None] * L_DEV + leaf_index[None, :])[:, :, None]
    table = jnp.concatenate([itself, nearby, remote], axis=2).reshape(NLEAF, NEAR)

    def pick_order(single_key):
        return jax.random.permutation(single_key, NEAR).astype(jnp.int32)
    column_order = jax.vmap(pick_order)(jax.random.split(key_order, NLEAF))
    return jnp.take_along_axis(table, column_order, axis=1).astype(jnp.int32)


def plant(array, stream_key, low, top_value):
    shape = array.shape
    place = [jax.random.randint(jax.random.fold_in(stream_key, axis), (), 0, shape[axis]) for axis in range(len(shape))]
    array = array.at[tuple(place)].set(low)
    longest = shape.index(max(shape))
    place[longest] = (place[longest] + 1) % shape[longest]
    return array.at[tuple(place)].set(top_value)


def levels(rng, shape, shards, least, largest):
    factor_of = 1.0
    for dim, shards_of in shards:
        draws = jax.random.uniform(jax.random.fold_in(jax.random.fold_in(rng, 6), dim), (shards_of,), jnp.float32, least / len(shards), largest / len(shards))
        factor_of = factor_of * jnp.repeat(jnp.exp(draws), shape[dim] // shards_of).reshape((-1,) + (1,) * (len(shape) - 1 - dim))
    return factor_of


def normal_values(stream_key, dims, deviation, bound, cuts=(), kind=jnp.bfloat16):
    entries = jax.random.normal(stream_key, dims, jnp.float32) * deviation
    if len(cuts) > 0:
        entries = levels(stream_key, dims, cuts, -0.22, 0.18) * entries
    return jnp.clip(entries, min=-bound, max=bound).astype(kind)


def setup_inputs(seed: int = 0) -> dict:
    arg_keys = jax.random.split(jax.random.key(seed), 11)
    return {
        "start": draw_start(jax.random.fold_in(arg_keys[10], 71), 0),
        "coords": jnp.clip(jax.random.uniform(arg_keys[1], (NLEAF, 3, LEAF), jnp.float32, -1.0, 1.0) * levels(arg_keys[1], (NLEAF, 3, LEAF), ((0, 32),), -0.4, 0.0), -1.0, 1.0),
        "area": jnp.clip(jnp.exp(math.log(0.4) - 1.3862944 * jax.random.uniform(arg_keys[2], (NLEAF, LEAF), jnp.float32) ** levels(arg_keys[2], (NLEAF, LEAF), ((0, 32),), -0.2, 0.2)), 0.1, 0.4),
        "near_list": draw_near_list(jax.random.fold_in(arg_keys[10], 71), 0),
        "basis": normal_values(arg_keys[4], (NLEAF, RANK, LEAF), LEAF ** -0.5, 0.375, ((0, 32),), jnp.float32),
        "far_leaf": plant(jax.random.randint(arg_keys[5], (NLEAF, FAR), 0, N_DEV * L_DEV), jax.random.fold_in(arg_keys[5], 1), 0, (N_DEV * L_DEV) - 1).astype(jnp.int32),
        "couple_leaf": normal_values(arg_keys[6], (NLEAF, RANK, FAR * RANK), (FAR * RANK) ** -0.5, 0.25, ((0, 32),), jnp.float32),
        "transfer": normal_values(arg_keys[7], (DEVICES, RANK, L_DEV * RANK), (4 * RANK) ** -0.5, 0.375, ((0, 32),), jnp.float32),
        "far_top": plant(jax.random.randint(arg_keys[8], (DEVICES, FAR_TOP), 0, DEVICES), jax.random.fold_in(arg_keys[8], 1), 0, DEVICES - 1).astype(jnp.int32),
        "couple_top": normal_values(arg_keys[9], (DEVICES, RANK, FAR_TOP * RANK), (FAR_TOP * RANK) ** -0.5, 0.1875, ((0, 32),), jnp.float32),
    }


FOUR_PI = 4.0 * math.pi
SOFTENING = 0.01
EPSILON = 1e-06
HIGHEST_PRECISION = lax.Precision.HIGHEST

def near_block(targets, sources, weights):
    squared = (targets[:, None, 0, :, None] - sources[:, :, 0, None, :]) ** 2
    for component in (1, 2):
        squared = squared + (targets[:, None, component, :, None] - sources[:, :, component, None, :]) ** 2
    coupling = 1.0 / (FOUR_PI * jnp.sqrt(squared + SOFTENING))
    return jnp.einsum('bkij,bkj->bi', coupling, weights, precision=HIGHEST_PRECISION)

def apply_operator(vector, coords, area, near_list, basis, far_leaf, couple_leaf, transfer, far_top, couple_top):
    charges = area * vector
    live = near_list >= 0
    safe_ids = jnp.where(live, near_list, 0).astype(jnp.int32)
    weighted = charges[safe_ids] * live[:, :, None].astype(jnp.float32)
    blocks = NLEAF // 32

    def block_sum(pieces):
        targets, block_ids, block_weights = pieces
        return near_block(targets, coords[block_ids], block_weights)
    near_part = lax.map(block_sum, (coords.reshape(blocks, 32, 3, LEAF), safe_ids.reshape(blocks, 32, NEAR), weighted.reshape(blocks, 32, NEAR, LEAF))).reshape(NLEAF, LEAF)
    moments = jnp.einsum('lrj,lj->lr', basis, charges, precision=HIGHEST_PRECISION)
    group_leaves = N_DEV * L_DEV
    group_start = jnp.arange(NLEAF, dtype=jnp.int32) // group_leaves * group_leaves
    partner_ids = (group_start[:, None] + far_leaf).astype(jnp.int32)
    partners = moments[partner_ids].reshape(NLEAF, FAR * RANK)
    local = jnp.einsum('lrq,lq->lr', couple_leaf, partners, precision=HIGHEST_PRECISION)
    clusters = jnp.einsum('drq,dq->dr', transfer, moments.reshape(DEVICES, L_DEV * RANK), precision=HIGHEST_PRECISION)
    level = jnp.einsum('drq,dq->dr', couple_top, clusters[far_top].reshape(DEVICES, FAR_TOP * RANK), precision=HIGHEST_PRECISION)
    down = jnp.einsum('drq,dr->dq', transfer, level, precision=HIGHEST_PRECISION).reshape(NLEAF, RANK)
    return near_part + jnp.einsum('lrj,lr->lj', basis, local + down, precision=HIGHEST_PRECISION)

def reference(start, coords, area, near_list, basis, far_leaf, couple_leaf, transfer, far_top, couple_top):
    operands = (coords, area, near_list, basis, far_leaf, couple_leaf, transfer, far_top, couple_top)
    squares_start = jnp.sum(start * start)
    unit_first = start / jnp.sqrt(squares_start / PANELS + EPSILON)
    product_first = apply_operator(unit_first, *operands)
    projection = jnp.sum(unit_first * product_first) / jnp.sum(unit_first * unit_first)
    orthogonal = product_first - projection * unit_first
    squares_second = jnp.sum(orthogonal * orthogonal)
    unit_second = orthogonal / jnp.sqrt(squares_second / PANELS + EPSILON)
    product_second = apply_operator(unit_second, *operands)
    return (product_first, product_second)
```

```python
import functools
import math

import jax
import jax.numpy as jnp
from jax import lax
from jax.experimental import pallas as pl
from jax.experimental.pallas import tpu as pltpu
from jax.sharding import PartitionSpec as P

FOUR_PI = 4.0 * math.pi
SOFTENING = 0.01
EPSILON = 1e-06
LIFT = 1024.0
MESH = pl.DeviceIdType.MESH
LANES = 128


def thirds(x):
    high = x.astype(jnp.bfloat16).astype(jnp.float32)
    rest = x - high
    middle = rest.astype(jnp.bfloat16).astype(jnp.float32)
    return high, middle, rest - middle


def kernel(
    devs, groups, near_ref, far_ref, top_ref, start_ref, coords_ref, area_ref, basis_ref,
    couple_ref, transfer_ref, ctop_ref, out1_ref, out2_ref, points, weights, weights2, moms,
    moms2, tops, tops2, norms, kmat, near_acc, down_ref, send_sem, recv_sem, xsend_sem, xrecv_sem,
):
    leaves, panels = start_ref.shape
    entries = near_ref.shape[1]
    coeffs = basis_ref.shape[1]
    fars = far_ref.shape[1]
    pairs = leaves // 2
    me = lax.axis_index("dev")
    grp = lax.axis_index("group")
    base = me * leaves

    def dev_peer(k):
        return (grp, lax.rem(me + k, devs))

    def grp_peer(k):
        return (lax.rem(grp + k, groups), me)

    barrier = pltpu.get_barrier_semaphore()

    def greet_dev(k, c):
        pl.semaphore_signal(barrier, inc=1, device_id=dev_peer(k), device_id_type=MESH)
        return c

    def greet_grp(k, c):
        pl.semaphore_signal(barrier, inc=1, device_id=grp_peer(k), device_id_type=MESH)
        return c

    lax.fori_loop(1, devs, greet_dev, 0)
    lax.fori_loop(1, groups, greet_grp, 0)
    pl.semaphore_wait(barrier, devs + groups - 2)

    def copy_in_group(phase, buf, first, rows, k):
        part = buf.at[pl.ds(first, rows)]
        return pltpu.make_async_remote_copy(
            src_ref=part, dst_ref=part, send_sem=send_sem.at[phase, k],
            recv_sem=recv_sem.at[phase, k], device_id=dev_peer(k), device_id_type=MESH,
        )

    def copy_across(phase, buf, k):
        part = buf.at[pl.ds(grp * devs, devs)]
        return pltpu.make_async_remote_copy(
            src_ref=part, dst_ref=part, send_sem=xsend_sem.at[phase, k],
            recv_sem=xrecv_sem.at[phase, k], device_id=grp_peer(k), device_id_type=MESH,
        )

    def in_group(phase, buf, per_dev, offset=0):
        first = offset + me * per_dev

        def start(k, c):
            copy_in_group(phase, buf, first, per_dev, k).start()
            return c

        def arrive(k, c):
            sender = lax.rem(me - k + devs, devs)
            copy_in_group(phase, buf, offset + sender * per_dev, per_dev, k).wait_recv()
            return c

        def sent(k, c):
            copy_in_group(phase, buf, first, per_dev, k).wait_send()
            return c

        return tuple(
            functools.partial(lax.fori_loop, 1, devs, f, 0) for f in (start, arrive, sent)
        )

    def across(phase, buf):
        def start(k, c):
            copy_across(phase, buf, k).start()
            return c

        def arrive(k, c):
            sender = lax.rem(grp - k + groups, groups)
            part = buf.at[pl.ds(sender * devs, devs)]
            pltpu.make_async_remote_copy(
                src_ref=part, dst_ref=part, send_sem=xsend_sem.at[phase, k],
                recv_sem=xrecv_sem.at[phase, k], device_id=grp_peer(k), device_id_type=MESH,
            ).wait_recv()
            return c

        def sent(k, c):
            copy_across(phase, buf, k).wait_send()
            return c

        return tuple(
            functools.partial(lax.fori_loop, 1, groups, f, 0) for f in (start, arrive, sent)
        )

    points_c = in_group(0, points, 3 * leaves)
    weights_c = in_group(1, weights, leaves)
    moms_c = in_group(2, moms, leaves)
    tops_c = in_group(3, tops, 1, grp * devs)
    weights2_c = in_group(4, weights2, leaves)
    moms2_c = in_group(5, moms2, leaves)
    tops2_c = in_group(6, tops2, 1, grp * devs)
    norms_c = in_group(7, norms, 1, grp * devs)
    tops_x = across(0, tops)
    tops2_x = across(1, tops2)
    norms_x = across(2, norms)

    lane = lax.broadcasted_iota(jnp.int32, (1, LANES), 1)
    low_half = lane < coeffs
    row_r = lax.broadcasted_iota(jnp.int32, (coeffs, LANES), 0)
    lane_r = lax.broadcasted_iota(jnp.int32, (coeffs, LANES), 1)
    twice_eye = lax.rem(lane_r, coeffs) == row_r
    row_p = lax.broadcasted_iota(jnp.int32, (LANES, LANES), 0)
    lane_p = lax.broadcasted_iota(jnp.int32, (LANES, LANES), 1)
    eye = row_p == lane_p
    row8 = lax.broadcasted_iota(jnp.int32, (8, panels), 0)

    def lane_sum(x):
        total = x[:, :LANES]
        for j in range(1, x.shape[1] // LANES):
            total = total + x[:, j * LANES:(j + 1) * LANES]
        return jnp.sum(total, axis=1, keepdims=True)

    def total_of(x):
        return jnp.sum(jnp.sum(x, axis=0, keepdims=True), axis=1, keepdims=True)

    def twice_row(column):
        return jnp.sum(jnp.where(twice_eye, column, 0.0), axis=0, keepdims=True)

    def find_moments(charges, table):
        def body(l, c):
            product = basis_ref[l] * charges[pl.ds(base + l, 1), :]
            table[pl.ds(base + l, 1), :] = twice_row(lane_sum(product))
            return c

        lax.fori_loop(0, leaves, body, 0)

    def find_cluster(table):
        total = jnp.zeros((coeffs, LANES), jnp.float32)
        for j in range(pairs):
            pair = jnp.where(
                low_half, table[pl.ds(base + 2 * j, 1), :], table[pl.ds(base + 2 * j + 1, 1), :]
            )
            total = total + transfer_ref[0, :, j * LANES:(j + 1) * LANES] * pair
        return twice_row(lane_sum(total))

    def find_down(clusters):
        total = jnp.zeros((coeffs, LANES), jnp.float32)
        for j in range(top_ref.shape[1] // 2):
            pair = jnp.where(
                low_half, clusters[top_ref[0, 2 * j]],
                pltpu.roll(clusters[top_ref[0, 2 * j + 1]], coeffs, 1),
            )
            total = total + ctop_ref[0, :, j * LANES:(j + 1) * LANES] * pair
        level = lane_sum(total)
        for j in range(pairs):
            down_ref[j:j + 1, :] = jnp.sum(
                transfer_ref[0, :, j * LANES:(j + 1) * LANES] * level, axis=0, keepdims=True
            )

    def far_row(l, table):
        half = lax.rem(l, 2) * coeffs
        total = jnp.where(lane_r == row_r + half, down_ref[pl.ds(l // 2, 1), :], 0.0)
        for j in range(fars // 2):
            pair = jnp.where(
                low_half, table[pl.ds(far_ref[l, 2 * j], 1), :],
                table[pl.ds(far_ref[l, 2 * j + 1], 1), :],
            )
            total = total + couple_ref[l, :, j * LANES:(j + 1) * LANES] * pair
        return jnp.sum(basis_ref[l] * lane_sum(total), axis=0, keepdims=True)

    def source_of(l, n):
        named = near_ref[l, n]
        live = named >= 0
        index = jnp.where(live, named - grp * (devs * leaves), base + l)
        index = jnp.clip(index, 0, devs * leaves - 1)
        return index, jnp.where(live, 1.0 / FOUR_PI, 0.0)

    def point_rows(index):
        return [points[pl.ds(3 * index + c, 1), :] for c in range(3)]

    def stack8(rows):
        total = jnp.zeros((8, panels), jnp.float32)
        for c, row in enumerate(rows):
            total = jnp.where(row8 == c, row, total)
        return total

    def to_row(acc):
        column = jnp.sum(acc, axis=1, keepdims=True)
        parts = [
            jnp.sum(
                jnp.where(eye, column[h * LANES:(h + 1) * LANES], 0.0), axis=0, keepdims=True
            )
            for h in range(panels // LANES)
        ]
        return jnp.concatenate(parts, axis=1)

    def take_points(l, c):
        for axis in range(3):
            points[pl.ds(3 * (base + l) + axis, 1), :] = coords_ref[l, axis:axis + 1, :]
        return c

    lax.fori_loop(0, leaves, take_points, 0)
    points_c[0]()
    weights[pl.ds(base, leaves), :] = area_ref[...] * (start_ref[...] * LIFT)
    weights_c[0]()
    find_moments(weights, moms)
    moms_c[0]()
    squares = total_of(start_ref[...] * start_ref[...])
    tops[grp * devs + me] = jnp.where(low_half, find_cluster(moms), squares)
    tops_c[0]()
    points_c[1]()
    weights_c[1]()
    tops_c[1]()
    tops_x[0]()

    def near_first(l, c):
        x, y, z = point_rows(base + l)
        size = x * x + y * y + z * z + SOFTENING
        high, middle, low = thirds(
            stack8((-2.0 * x, -2.0 * y, -2.0 * z, size, jnp.ones_like(x)))
        )
        targets = jnp.concatenate((high, high, middle, middle, high, low), axis=0)
        targets = jnp.transpose(targets).astype(jnp.bfloat16)
        acc = jnp.zeros((panels, LANES), jnp.float32)
        for n in range(entries):
            index, scale = source_of(l, n)
            x, y, z = point_rows(index)
            high, middle, low = thirds(
                stack8((x, y, z, jnp.ones_like(x), x * x + y * y + z * z))
            )
            sources = jnp.concatenate((high, middle, high, middle, low, high), axis=0)
            squared = jnp.dot(
                targets, sources.astype(jnp.bfloat16), preferred_element_type=jnp.float32
            )
            coupling = lax.rsqrt(squared)
            kmat[l * entries + n] = coupling
            row = weights[pl.ds(index, 1), :] * scale
            for h in range(panels // LANES):
                cut = slice(h * LANES, (h + 1) * LANES)
                acc = acc + coupling[:, cut] * row[:, cut]
        near_acc[pl.ds(l, 1), :] = to_row(acc)
        return c

    lax.fori_loop(0, leaves, near_first, 0)
    moms_c[1]()
    tops_x[1]()
    find_down(tops)

    panels_all = float(leaves * panels * devs * groups)

    def scale_of(total):
        return 1.0 / jnp.sqrt(total / panels_all + EPSILON)

    def pick(row, at):
        return jnp.sum(jnp.where(lane == at, row, 0.0), axis=1, keepdims=True)

    first_scale = scale_of(pick(jnp.sum(tops[...], axis=0), coeffs))

    def far_first(l, c):
        near_acc[pl.ds(l, 1), :] = near_acc[pl.ds(l, 1), :] + far_row(l, moms)
        return c

    lax.fori_loop(0, leaves, far_first, 0)
    product = near_acc[...] * (first_scale * (1.0 / LIFT))
    unit = start_ref[...] * first_scale
    out1_ref[...] = product
    weights2[pl.ds(base, leaves), :] = area_ref[...] * product
    weights2_c[0]()
    find_moments(weights2, moms2)
    moms2_c[0]()
    along = total_of(unit * product)
    length = total_of(unit * unit)
    sums = jnp.where(lane < coeffs + coeffs // 2, along, length)
    tops2[grp * devs + me] = jnp.where(low_half, find_cluster(moms2), sums)
    tops2_c[0]()
    weights2_c[1]()
    tops2_c[1]()
    tops2_x[0]()

    def near_second(l, c):
        acc = jnp.zeros((panels, LANES), jnp.float32)
        for n in range(entries):
            index, scale = source_of(l, n)
            row = weights2[pl.ds(index, 1), :] * scale
            for h in range(panels // LANES):
                cut = slice(h * LANES, (h + 1) * LANES)
                acc = acc + kmat[l * entries + n, :, cut] * row[:, cut]
        near_acc[pl.ds(l, 1), :] = to_row(acc)
        return c

    some = leaves // 2
    lax.fori_loop(0, some, near_second, 0)
    tops2_x[1]()
    sums = jnp.sum(tops2[...], axis=0)
    projection = pick(sums, coeffs) / pick(sums, coeffs + coeffs // 2)
    product = out1_ref[...]
    orthogonal = product - projection * (start_ref[...] * first_scale)
    norms[grp * devs + me] = jnp.broadcast_to(total_of(orthogonal * orthogonal), (1, LANES))
    norms_c[0]()
    lax.fori_loop(some, leaves, near_second, 0)
    norms_c[1]()
    norms_x[0]()
    moms2_c[1]()
    find_down(tops2)

    def far_second(l, c):
        near_acc[pl.ds(l, 1), :] = near_acc[pl.ds(l, 1), :] + far_row(l, moms2)
        return c

    lax.fori_loop(0, leaves, far_second, 0)
    norms_x[1]()
    second_scale = scale_of(pick(jnp.sum(norms[...], axis=0), 0))
    out2_ref[...] = (near_acc[...] - projection * out1_ref[...]) * second_scale

    for copies in (
        points_c, weights_c, moms_c, tops_c, weights2_c, moms2_c, tops2_c, norms_c,
        tops_x, tops2_x, norms_x,
    ):
        copies[2]()


def per_device(
    start, coords, area, near_list, basis, far_leaf, couple_leaf, transfer, far_top, couple_top
):
    leaves, panels = start.shape
    entries = near_list.shape[1]
    devs = lax.axis_size("dev")
    groups = lax.axis_size("group")
    smem = pl.BlockSpec(memory_space=pltpu.SMEM)
    vmem = pl.BlockSpec(memory_space=pltpu.VMEM)
    f32 = jnp.float32
    return tuple(pl.pallas_call(
        functools.partial(kernel, devs, groups),
        out_shape=[jax.ShapeDtypeStruct((leaves, panels), f32)] * 2,
        in_specs=[smem] * 3 + [vmem] * 7,
        out_specs=[vmem] * 2,
        scratch_shapes=[
            pltpu.VMEM((devs * leaves * 3, panels), f32),
            pltpu.VMEM((devs * leaves, panels), f32),
            pltpu.VMEM((devs * leaves, panels), f32),
            pltpu.VMEM((devs * leaves, LANES), f32),
            pltpu.VMEM((devs * leaves, LANES), f32),
            pltpu.VMEM((groups * devs, 1, LANES), f32),
            pltpu.VMEM((groups * devs, 1, LANES), f32),
            pltpu.VMEM((groups * devs, 1, LANES), f32),
            pltpu.VMEM((leaves * entries, panels, panels), f32),
            pltpu.VMEM((leaves, panels), f32),
            pltpu.VMEM((leaves // 2, LANES), f32),
            pltpu.SemaphoreType.DMA((8, devs)),
            pltpu.SemaphoreType.DMA((8, devs)),
            pltpu.SemaphoreType.DMA((3, groups)),
            pltpu.SemaphoreType.DMA((3, groups)),
        ],
        compiler_params=pltpu.CompilerParams(
            collective_id=0, has_side_effects=True, vmem_limit_bytes=48 * 1024 * 1024
        ),
    )(near_list, far_leaf, far_top, start, coords, area, basis, couple_leaf, transfer, couple_top))


def solution(mesh):
    rows = P(("group", "dev"), None)
    blocks = P(("group", "dev"), None, None)
    in_specs = (rows, blocks, rows, rows, blocks, rows, blocks, blocks, rows, blocks)
    return jax.shard_map(
        per_device, mesh=mesh, in_specs=in_specs, out_specs=(rows, rows), check_vma=False
    )
```

```python
import functools
import math

import jax
import jax.numpy as jnp
from jax import lax
from jax.experimental import pallas as pl
from jax.experimental.pallas import tpu as pltpu
from jax.sharding import PartitionSpec as P

FOUR_PI = 4.0 * math.pi
SOFTENING = 0.01
EPSILON = 1e-06
LIFT = 1024.0
MESH = pl.DeviceIdType.MESH
LANES = 128


def thirds(x):
    high = x.astype(jnp.bfloat16).astype(jnp.float32)
    rest = x - high
    middle = rest.astype(jnp.bfloat16).astype(jnp.float32)
    return high, middle, rest - middle


def kernel(
    devs, groups, near_ref, far_ref, top_ref, start_hbm, coords_hbm, area_hbm, basis_hbm,
    couple_hbm, transfer_hbm, ctop_hbm, out_ref, start_ref, area_ref, basis_ref, couple_ref,
    transfer_ref, ctop_ref, points, parcel, parcel2, tops, tops2, kmat, near_acc, down_ref,
    load_sem, send_sem, recv_sem, xsend_sem, xrecv_sem,
):
    leaves, panels = start_ref.shape
    entries = near_ref.shape[0]
    coeffs = basis_ref.shape[1]
    fars = far_ref.shape[0]
    pairs = leaves // 2
    halves = panels // LANES
    mom_row = halves * leaves
    top_row = mom_row + leaves
    me = lax.axis_index("dev")
    grp = lax.axis_index("group")

    def dev_peer(k):
        return (grp, lax.rem(me + k, devs))

    def grp_peer(k):
        return (lax.rem(grp + k, groups), me)

    barrier = pltpu.get_barrier_semaphore()

    def greet_dev(k, c):
        pl.semaphore_signal(barrier, inc=1, device_id=dev_peer(k), device_id_type=MESH)
        return c

    def greet_grp(k, c):
        pl.semaphore_signal(barrier, inc=1, device_id=grp_peer(k), device_id_type=MESH)
        return c

    lax.fori_loop(1, devs, greet_dev, 0)
    lax.fori_loop(1, groups, greet_grp, 0)

    loads = [
        pltpu.make_async_copy(source, target, load_sem.at[n])
        for n, (source, target) in enumerate((
            (start_hbm, start_ref), (area_hbm, area_ref), (basis_hbm, basis_ref),
            (transfer_hbm, transfer_ref), (coords_hbm, points.at[me]), (ctop_hbm, ctop_ref),
            (couple_hbm, couple_ref),
        ))
    ]
    for load in loads:
        load.start()

    def in_group(phase, buf, first):
        def copy(source, block, k):
            return pltpu.make_async_remote_copy(
                src_ref=source, dst_ref=buf.at[block], send_sem=send_sem.at[phase, k],
                recv_sem=recv_sem.at[phase, k], device_id=dev_peer(k), device_id_type=MESH,
            )

        def start(k, c):
            copy(first, me, k).start()
            return c

        def arrive(k, c):
            sender = lax.rem(me - k + devs, devs)
            copy(buf.at[sender], sender, k).wait_recv()
            return c

        def sent(k, c):
            copy(first, me, k).wait_send()
            return c

        return tuple(
            functools.partial(lax.fori_loop, 1, devs, f, 0) for f in (start, arrive, sent)
        )

    def across(phase, buf):
        def copy(block, k):
            part = buf.at[pl.ds(block * devs, devs)]
            return pltpu.make_async_remote_copy(
                src_ref=part, dst_ref=part, send_sem=xsend_sem.at[phase, k],
                recv_sem=xrecv_sem.at[phase, k], device_id=grp_peer(k), device_id_type=MESH,
            )

        def start(k, c):
            copy(grp, k).start()
            return c

        def arrive(k, c):
            copy(lax.rem(grp - k + groups, groups), k).wait_recv()
            return c

        def sent(k, c):
            copy(grp, k).wait_send()
            return c

        return tuple(
            functools.partial(lax.fori_loop, 1, groups, f, 0) for f in (start, arrive, sent)
        )

    points_c = in_group(0, points, coords_hbm)
    parcel_c = in_group(1, parcel, parcel.at[me])
    parcel2_c = in_group(2, parcel2, parcel2.at[me])
    tops_x = across(0, tops)
    tops2_x = across(1, tops2)

    lane = lax.broadcasted_iota(jnp.int32, (1, LANES), 1)
    low_half = lane < coeffs
    row_r = lax.broadcasted_iota(jnp.int32, (coeffs, LANES), 0)
    lane_r = lax.broadcasted_iota(jnp.int32, (coeffs, LANES), 1)
    twice_eye = lax.rem(lane_r, coeffs) == row_r
    row_p = lax.broadcasted_iota(jnp.int32, (LANES, LANES), 0)
    lane_p = lax.broadcasted_iota(jnp.int32, (LANES, LANES), 1)
    eye = row_p == lane_p
    row8 = lax.broadcasted_iota(jnp.int32, (8, panels), 0)

    def lane_sum(x):
        total = x[:, :LANES]
        for j in range(1, x.shape[1] // LANES):
            total = total + x[:, j * LANES:(j + 1) * LANES]
        return jnp.sum(total, axis=1, keepdims=True)

    def total_of(x):
        return jnp.sum(jnp.sum(x, axis=0, keepdims=True), axis=1, keepdims=True)

    def twice_row(column):
        return jnp.sum(jnp.where(twice_eye, column, 0.0), axis=0, keepdims=True)

    def moment_row(table, index):
        return table[index // leaves, pl.ds(mom_row + lax.rem(index, leaves), 1), :]

    def pack(table, charges, sums):
        for h in range(halves):
            table[me, h * leaves:(h + 1) * leaves, :] = charges[:, h * LANES:(h + 1) * LANES]

        def body(l, c):
            total = jnp.zeros((coeffs, LANES), jnp.float32)
            for h in range(halves):
                row = table[me, pl.ds(h * leaves + l, 1), :]
                total = total + basis_ref[l, :, h * LANES:(h + 1) * LANES] * row
            table[me, pl.ds(mom_row + l, 1), :] = twice_row(lane_sum(total))
            return c

        lax.fori_loop(0, leaves, body, 0)
        total = jnp.zeros((coeffs, LANES), jnp.float32)
        for j in range(pairs):
            row = mom_row + 2 * j
            pair = jnp.where(low_half, table[me, row:row + 1, :], table[me, row + 1:row + 2, :])
            total = total + transfer_ref[0, :, j * LANES:(j + 1) * LANES] * pair
        cluster = jnp.where(low_half, twice_row(lane_sum(total)), sums)
        table[me, top_row:top_row + 8, :] = jnp.broadcast_to(cluster, (8, LANES))

    def collect_tops(table, clusters):
        def body(d, c):
            clusters[grp * devs + d] = table[d, top_row:top_row + 1, :]
            return c

        lax.fori_loop(0, devs, body, 0)

    def find_down(clusters):
        total = jnp.zeros((coeffs, LANES), jnp.float32)
        for j in range(top_ref.shape[1] // 2):
            pair = jnp.where(
                low_half, clusters[top_ref[0, 2 * j]],
                pltpu.roll(clusters[top_ref[0, 2 * j + 1]], coeffs, 1),
            )
            total = total + ctop_ref[0, :, j * LANES:(j + 1) * LANES] * pair
        level = lane_sum(total)
        for j in range(pairs):
            down_ref[j:j + 1, :] = jnp.sum(
                transfer_ref[0, :, j * LANES:(j + 1) * LANES] * level, axis=0, keepdims=True
            )

    def far_row(l, table):
        half = lax.rem(l, 2) * coeffs
        total = jnp.where(lane_r == row_r + half, down_ref[pl.ds(l // 2, 1), :], 0.0)
        for j in range(fars // 2):
            pair = jnp.where(
                low_half, moment_row(table, far_ref[2 * j, l]), moment_row(table, far_ref[2 * j + 1, l])
            )
            total = total + couple_ref[l, :, j * LANES:(j + 1) * LANES] * pair
        return jnp.sum(basis_ref[l] * lane_sum(total), axis=0, keepdims=True)

    def source_of(l, n):
        named = near_ref[n, l]
        live = named >= 0
        index = jnp.where(live, named - grp * (devs * leaves), me * leaves + l)
        index = jnp.clip(index, 0, devs * leaves - 1)
        return index, jnp.where(live, 1.0 / FOUR_PI, 0.0)

    def point_rows(index):
        device, leaf = index // leaves, lax.rem(index, leaves)
        return [points[device, c, pl.ds(leaf, 1), :] for c in range(3)]

    def charge_rows(table, index, scale):
        device, leaf = index // leaves, lax.rem(index, leaves)
        return [
            table[device, pl.ds(h * leaves + leaf, 1), :] * scale for h in range(halves)
        ]

    def stack8(rows):
        total = jnp.zeros((8, panels), jnp.float32)
        for c, row in enumerate(rows):
            total = jnp.where(row8 == c, row, total)
        return total

    def to_row(acc):
        column = jnp.sum(acc, axis=1, keepdims=True)
        parts = [
            jnp.sum(
                jnp.where(eye, column[h * LANES:(h + 1) * LANES], 0.0), axis=0, keepdims=True
            )
            for h in range(panels // LANES)
        ]
        return jnp.concatenate(parts, axis=1)

    loads[0].wait()
    loads[1].wait()
    squares = total_of(start_ref[...] * start_ref[...])
    pl.semaphore_wait(barrier, devs + groups - 2)
    points_c[0]()
    loads[2].wait()
    loads[3].wait()
    pack(parcel, area_ref[...] * (start_ref[...] * LIFT), squares)
    parcel_c[0]()
    loads[4].wait()
    points_c[1]()
    parcel_c[1]()
    collect_tops(parcel, tops)
    tops_x[0]()

    def near_first(l, c):
        x, y, z = point_rows(me * leaves + l)
        size = x * x + y * y + z * z + SOFTENING
        high, middle, low = thirds(
            stack8((-2.0 * x, -2.0 * y, -2.0 * z, size, jnp.ones_like(x)))
        )
        targets = jnp.concatenate((high, high, middle, middle, high, low), axis=0)
        targets = jnp.transpose(targets).astype(jnp.bfloat16)
        acc = jnp.zeros((panels, LANES), jnp.float32)
        for n in range(entries):
            index, scale = source_of(l, n)
            x, y, z = point_rows(index)
            high, middle, low = thirds(
                stack8((x, y, z, jnp.ones_like(x), x * x + y * y + z * z))
            )
            sources = jnp.concatenate((high, middle, high, middle, low, high), axis=0)
            squared = jnp.dot(
                targets, sources.astype(jnp.bfloat16), preferred_element_type=jnp.float32
            )
            coupling = lax.rsqrt(squared)
            kmat[l * entries + n] = coupling
            for h, row in enumerate(charge_rows(parcel, index, scale)):
                acc = acc + coupling[:, h * LANES:(h + 1) * LANES] * row
        near_acc[pl.ds(l, 1), :] = to_row(acc)
        return c

    lax.fori_loop(0, leaves, near_first, 0)
    tops_x[1]()
    loads[5].wait()
    loads[6].wait()
    find_down(tops)

    panels_all = float(leaves * panels * devs * groups)

    def scale_of(total):
        return 1.0 / jnp.sqrt(total / panels_all + EPSILON)

    def pick(row, at):
        return jnp.sum(jnp.where(lane == at, row, 0.0), axis=1, keepdims=True)

    first_scale = scale_of(pick(jnp.sum(tops[...], axis=0), coeffs))

    def far_first(l, c):
        near_acc[pl.ds(l, 1), :] = near_acc[pl.ds(l, 1), :] + far_row(l, parcel)
        return c

    lax.fori_loop(0, leaves, far_first, 0)
    product = near_acc[...] * (first_scale * (1.0 / LIFT))
    unit = start_ref[...] * first_scale
    out_ref[0] = product
    along = total_of(unit * product)
    length = total_of(unit * unit)
    part = jnp.where(length > 0.0, along / length, 0.0)
    beyond = total_of((product - part * unit) ** 2)
    sums = jnp.where(
        lane == coeffs, along, jnp.where(lane == coeffs + 1, length, jnp.where(
            lane == coeffs + 2, beyond, part
        ))
    )
    pack(parcel2, area_ref[...] * product, sums)
    parcel2_c[0]()
    parcel2_c[1]()
    collect_tops(parcel2, tops2)
    tops2_x[0]()

    def near_second(l, c):
        acc = jnp.zeros((panels, LANES), jnp.float32)
        for n in range(entries):
            index, scale = source_of(l, n)
            for h, row in enumerate(charge_rows(parcel2, index, scale)):
                acc = acc + kmat[l * entries + n, :, h * LANES:(h + 1) * LANES] * row
        near_acc[pl.ds(l, 1), :] = to_row(acc)
        return c

    lax.fori_loop(0, leaves, near_second, 0)
    tops2_x[1]()
    find_down(tops2)
    rows = tops2[...].reshape(groups * devs, LANES)

    def column(at):
        return jnp.sum(jnp.where(lane == at, rows, 0.0), axis=1, keepdims=True)

    lengths = column(coeffs + 1)
    projection = total_of(column(coeffs)) / total_of(lengths)
    beyond = total_of(column(coeffs + 2) + (column(coeffs + 3) - projection) ** 2 * lengths)
    second_scale = scale_of(beyond)

    def far_second(l, c):
        near_acc[pl.ds(l, 1), :] = near_acc[pl.ds(l, 1), :] + far_row(l, parcel2)
        return c

    lax.fori_loop(0, leaves, far_second, 0)
    out_ref[1] = (near_acc[...] - projection * out_ref[0]) * second_scale

    for copies in (points_c, parcel_c, parcel2_c, tops_x, tops2_x):
        copies[2]()


def per_device(
    start, coords, area, near_list, basis, far_leaf, couple_leaf, transfer, far_top, couple_top
):
    leaves, panels = start.shape
    entries = near_list.shape[1]
    devs = lax.axis_size("dev")
    groups = lax.axis_size("group")
    smem = pl.BlockSpec(memory_space=pltpu.SMEM)
    anywhere = pl.BlockSpec(memory_space=pl.ANY)
    f32 = jnp.float32
    parcel_rows = panels // LANES * leaves + leaves + 8
    both = pl.pallas_call(
        functools.partial(kernel, devs, groups),
        out_shape=jax.ShapeDtypeStruct((2, leaves, panels), f32),
        in_specs=[smem] * 3 + [anywhere] * 7,
        out_specs=pl.BlockSpec(memory_space=pltpu.VMEM),
        scratch_shapes=[
            pltpu.VMEM(start.shape, f32),
            pltpu.VMEM(area.shape, f32),
            pltpu.VMEM(basis.shape, f32),
            pltpu.VMEM(couple_leaf.shape, f32),
            pltpu.VMEM(transfer.shape, f32),
            pltpu.VMEM(couple_top.shape, f32),
            pltpu.VMEM((devs, 3, leaves, panels), f32),
            pltpu.VMEM((devs, parcel_rows, LANES), f32),
            pltpu.VMEM((devs, parcel_rows, LANES), f32),
            pltpu.VMEM((groups * devs, 1, LANES), f32),
            pltpu.VMEM((groups * devs, 1, LANES), f32),
            pltpu.VMEM((leaves * entries, panels, panels), f32),
            pltpu.VMEM((leaves, panels), f32),
            pltpu.VMEM((leaves // 2, LANES), f32),
            pltpu.SemaphoreType.DMA((7,)),
            pltpu.SemaphoreType.DMA((3, devs)),
            pltpu.SemaphoreType.DMA((3, devs)),
            pltpu.SemaphoreType.DMA((2, groups)),
            pltpu.SemaphoreType.DMA((2, groups)),
        ],
        compiler_params=pltpu.CompilerParams(
            collective_id=0, has_side_effects=True, vmem_limit_bytes=60 * 1024 * 1024
        ),
    )(
        near_list.T, far_leaf.T, far_top, start, jnp.transpose(coords, (1, 0, 2)), area, basis,
        couple_leaf, transfer, couple_top,
    )
    return both[0], both[1]


def solution(mesh):
    rows = P(("group", "dev"), None)
    blocks = P(("group", "dev"), None, None)
    in_specs = (rows, blocks, rows, rows, blocks, rows, blocks, blocks, rows, blocks)
    return jax.shard_map(
        per_device, mesh=mesh, in_specs=in_specs, out_specs=(rows, rows), check_vma=False
    )
```

```python
import functools
import math

import jax
import jax.numpy as jnp
from jax import lax
from jax.experimental import pallas as pl
from jax.experimental.pallas import tpu as pltpu
from jax.sharding import PartitionSpec as P

FOUR_PI = 4.0 * math.pi
SOFTENING = 0.01
EPSILON = 1e-06
LIFT = 1024.0
MESH = pl.DeviceIdType.MESH
LANES = 128


def thirds(x):
    high = x.astype(jnp.bfloat16).astype(jnp.float32)
    rest = x - high
    middle = rest.astype(jnp.bfloat16).astype(jnp.float32)
    return high, middle, rest - middle


def kernel(
    devs, groups, near_ref, far_ref, top_ref, start_hbm, coords_hbm, area_hbm, basis_hbm,
    couple_hbm, transfer_hbm, ctop_hbm, out_ref, start_ref, area_ref, basis_ref, couple_ref,
    transfer_ref, ctop_ref, points, parcel, parcel2, tops, tops2, kmat, near_acc, down_ref,
    moms, locs, aims, load_sem, send_sem, recv_sem, xsend_sem, xrecv_sem,
):
    leaves, panels = start_ref.shape
    entries = near_ref.shape[0]
    coeffs = basis_ref.shape[1]
    fars = far_ref.shape[0]
    pairs = leaves // 2
    halves = panels // LANES
    mom_row = halves * leaves
    me = lax.axis_index("dev")
    grp = lax.axis_index("group")

    def dev_peer(k):
        return (grp, lax.rem(me + k, devs))

    def grp_peer(k):
        return (lax.rem(grp + k, groups), me)

    barrier = pltpu.get_barrier_semaphore()

    def greet_dev(k, c):
        pl.semaphore_signal(barrier, inc=1, device_id=dev_peer(k), device_id_type=MESH)
        return c

    def greet_grp(k, c):
        pl.semaphore_signal(barrier, inc=1, device_id=grp_peer(k), device_id_type=MESH)
        return c

    lax.fori_loop(1, devs, greet_dev, 0)
    lax.fori_loop(1, groups, greet_grp, 0)

    loads = [
        pltpu.make_async_copy(source, target, load_sem.at[n])
        for n, (source, target) in enumerate((
            (start_hbm, start_ref), (area_hbm, area_ref), (basis_hbm, basis_ref),
            (transfer_hbm, transfer_ref), (coords_hbm, points.at[me]), (ctop_hbm, ctop_ref),
            (couple_hbm, couple_ref),
        ))
    ]
    for load in loads:
        load.start()

    def exchange(sems, count, mine, peer, source, block):
        send, recv = sems

        def copy(src, dst, k):
            return pltpu.make_async_remote_copy(
                src_ref=src, dst_ref=dst, send_sem=send(k), recv_sem=recv(k),
                device_id=peer(k), device_id_type=MESH,
            )

        def start(k, c):
            copy(source, block(mine), k).start()
            return c

        def arrive(k, c):
            landed = block(lax.rem(mine - k + count, count))
            copy(landed, landed, k).wait_recv()
            return c

        def sent(k, c):
            copy(source, block(mine), k).wait_send()
            return c

        return tuple(
            functools.partial(lax.fori_loop, 1, count, f, 0) for f in (start, arrive, sent)
        )

    def in_group(phase, source, block):
        sems = (lambda k: send_sem.at[phase, k], lambda k: recv_sem.at[phase, k])
        return exchange(sems, devs, me, dev_peer, source, block)

    def across(phase, buf):
        sems = (lambda k: xsend_sem.at[phase, k], lambda k: xrecv_sem.at[phase, k])
        return exchange(
            sems, groups, grp, grp_peer, buf.at[me * groups + grp],
            lambda g: buf.at[me * groups + g],
        )

    def line(buf):
        return lambda d: buf.at[pl.ds(d * groups, groups)]

    points_c = in_group(0, coords_hbm, lambda d: points.at[d])
    parcel_c = in_group(1, parcel.at[me], lambda d: parcel.at[d])
    parcel2_c = in_group(2, parcel2.at[me], lambda d: parcel2.at[d])
    tops_c = in_group(3, line(tops)(me), line(tops))
    tops2_c = in_group(4, line(tops2)(me), line(tops2))
    tops_x = across(0, tops)
    tops2_x = across(1, tops2)

    lane = lax.broadcasted_iota(jnp.int32, (1, LANES), 1)
    low_half = lane < coeffs
    row_r = lax.broadcasted_iota(jnp.int32, (coeffs, LANES), 0)
    lane_r = lax.broadcasted_iota(jnp.int32, (coeffs, LANES), 1)
    twice_eye = lax.rem(lane_r, coeffs) == row_r
    row_p = lax.broadcasted_iota(jnp.int32, (LANES, LANES), 0)
    lane_p = lax.broadcasted_iota(jnp.int32, (LANES, LANES), 1)
    eye = row_p == lane_p
    row8 = lax.broadcasted_iota(jnp.int32, (8, panels), 0)

    def lane_sum(x):
        total = x[:, :LANES]
        for j in range(1, x.shape[1] // LANES):
            total = total + x[:, j * LANES:(j + 1) * LANES]
        return jnp.sum(total, axis=1, keepdims=True)

    def total_of(x):
        return jnp.sum(jnp.sum(x, axis=0, keepdims=True), axis=1, keepdims=True)

    def twice_row(column):
        return jnp.sum(jnp.where(twice_eye, column, 0.0), axis=0, keepdims=True)

    def moment_row(index):
        return moms[index // leaves, pl.ds(lax.rem(index, leaves), 1), :]

    def pack(table, clusters, charges, sums):
        for h in range(halves):
            table[me, h * leaves:(h + 1) * leaves, :] = charges[:, h * LANES:(h + 1) * LANES]

        def body(i, c):
            rows = []
            for q in range(4):
                l = 4 * i + q
                total = jnp.zeros((coeffs, LANES), jnp.float32)
                for h in range(halves):
                    row = table[me, pl.ds(h * leaves + l, 1), :]
                    total = total + basis_ref[l, :, h * LANES:(h + 1) * LANES] * row
                rows.append(twice_row(lane_sum(total)))
            for q in range(4):
                moms[me, pl.ds(4 * i + q, 1), :] = rows[q]
            return c

        lax.fori_loop(0, leaves // 4, body, 0)
        table[me, mom_row:mom_row + pairs, :] = jnp.where(
            low_half, moms[me, :pairs, :], moms[me, pairs:, :]
        )
        total = jnp.zeros((coeffs, LANES), jnp.float32)
        for j in range(pairs):
            pair = jnp.where(
                low_half, moms[me, 2 * j:2 * j + 1, :], moms[me, 2 * j + 1:2 * j + 2, :]
            )
            total = total + transfer_ref[0, :, j * LANES:(j + 1) * LANES] * pair
        clusters[me * groups + grp] = jnp.where(low_half, twice_row(lane_sum(total)), sums)

    def unpack(table):
        def body(d, c):
            both = table[d, mom_row:mom_row + pairs, :]
            turned = pltpu.roll(both, coeffs, 1)
            moms[d, :pairs, :] = jnp.where(low_half, both, turned)
            moms[d, pairs:, :] = jnp.where(low_half, turned, both)
            return c

        lax.fori_loop(0, devs, body, 0)

    def cluster_row(clusters, index):
        return clusters[lax.rem(index, devs) * groups + index // devs]

    def find_down(clusters):
        total = jnp.zeros((coeffs, LANES), jnp.float32)
        for j in range(top_ref.shape[1] // 2):
            pair = jnp.where(
                low_half, cluster_row(clusters, top_ref[0, 2 * j]),
                pltpu.roll(cluster_row(clusters, top_ref[0, 2 * j + 1]), coeffs, 1),
            )
            total = total + ctop_ref[0, :, j * LANES:(j + 1) * LANES] * pair
        level = lane_sum(total)
        for j in range(pairs):
            down_ref[j:j + 1, :] = jnp.sum(
                transfer_ref[0, :, j * LANES:(j + 1) * LANES] * level, axis=0, keepdims=True
            )

    def find_local(l):
        total = jnp.zeros((coeffs, LANES), jnp.float32)
        for j in range(fars // 2):
            pair = jnp.where(
                low_half, moment_row(far_ref[2 * j, l]), moment_row(far_ref[2 * j + 1, l])
            )
            total = total + couple_ref[l, :, j * LANES:(j + 1) * LANES] * pair
        locs[l] = total

    def add_far(i, c):
        rows = []
        for q in range(4):
            l = 4 * i + q
            half = (q % 2) * coeffs
            down = down_ref[pl.ds(2 * i + q // 2, 1), :]
            total = locs[l] + jnp.where(lane_r == row_r + half, down, 0.0)
            rows.append(jnp.sum(basis_ref[l] * lane_sum(total), axis=0, keepdims=True))
        for q in range(4):
            at = pl.ds(4 * i + q, 1)
            near_acc[at, :] = near_acc[at, :] + rows[q]
        return c

    def source_of(l, n):
        own = (grp * devs + me) * leaves + l
        named = near_ref[n, l]
        named = jnp.where(named == own, near_ref[entries - 1, l], named)
        live = named >= 0
        index = jnp.where(live, named - grp * (devs * leaves), me * leaves + l)
        index = jnp.clip(index, 0, devs * leaves - 1)
        return index, jnp.where(live, 1.0 / FOUR_PI, 0.0)

    def point_rows(index):
        device, leaf = index // leaves, lax.rem(index, leaves)
        return [points[device, c, pl.ds(leaf, 1), :] for c in range(3)]

    def charge_rows(table, index, scale):
        device, leaf = index // leaves, lax.rem(index, leaves)
        return [
            table[device, pl.ds(h * leaves + leaf, 1), :] * scale for h in range(halves)
        ]

    def stack8(rows):
        total = jnp.zeros((8, panels), jnp.float32)
        for c, row in enumerate(rows):
            total = jnp.where(row8 == c, row, total)
        return total

    def to_row(acc):
        column = jnp.sum(acc, axis=1, keepdims=True)
        parts = [
            jnp.sum(
                jnp.where(eye, column[h * LANES:(h + 1) * LANES], 0.0), axis=0, keepdims=True
            )
            for h in range(panels // LANES)
        ]
        return jnp.concatenate(parts, axis=1)

    def sources_of(rows):
        x, y, z = rows
        high, middle, low = thirds(stack8((x, y, z, jnp.ones_like(x), x * x + y * y + z * z)))
        stacked = jnp.concatenate((high, middle, high, middle, low, high), axis=0)
        return stacked.astype(jnp.bfloat16)

    def coupling_of(targets, sources):
        return lax.rsqrt(jnp.dot(targets, sources, preferred_element_type=jnp.float32))

    loads[0].wait()
    loads[1].wait()
    squares = total_of(start_ref[...] * start_ref[...])
    pl.semaphore_wait(barrier, devs + groups - 2)
    points_c[0]()
    loads[2].wait()
    loads[3].wait()
    pack(parcel, tops, area_ref[...] * (start_ref[...] * LIFT), squares)
    parcel_c[0]()
    tops_x[0]()
    loads[4].wait()

    def near_self(l, c):
        rows = [points[me, axis, pl.ds(l, 1), :] for axis in range(3)]
        x, y, z = rows
        size = x * x + y * y + z * z + SOFTENING
        high, middle, low = thirds(
            stack8((-2.0 * x, -2.0 * y, -2.0 * z, size, jnp.ones_like(x)))
        )
        targets = jnp.concatenate((high, high, middle, middle, high, low), axis=0)
        targets = jnp.transpose(targets).astype(jnp.bfloat16)
        aims[l] = targets
        kmat[l * entries + entries - 1] = coupling_of(targets, sources_of(rows))
        return c

    lax.fori_loop(0, leaves, near_self, 0)
    tops_x[1]()
    tops_c[0]()
    loads[5].wait()
    loads[6].wait()
    points_c[1]()
    parcel_c[1]()
    unpack(parcel)

    def own_rows(table, l):
        return [
            table[me, pl.ds(h * leaves + l, 1), :] * (1.0 / FOUR_PI) for h in range(halves)
        ]

    def spread(acc, coupling, rows):
        for h, row in enumerate(rows):
            acc = acc + coupling[:, h * LANES:(h + 1) * LANES] * row
        return acc

    def near_first(l, c):
        acc = jnp.zeros((panels, LANES), jnp.float32)
        for n in range(entries - 1):
            index, scale = source_of(l, n)
            coupling = coupling_of(aims[l], sources_of(point_rows(index)))
            kmat[l * entries + n] = coupling
            acc = spread(acc, coupling, charge_rows(parcel, index, scale))
        acc = spread(acc, kmat[l * entries + entries - 1], own_rows(parcel, l))
        near_acc[pl.ds(l, 1), :] = to_row(acc)
        find_local(l)
        return c

    lax.fori_loop(0, leaves, near_first, 0)
    tops_c[1]()
    find_down(tops)

    panels_all = float(leaves * panels * devs * groups)

    def scale_of(total):
        return 1.0 / jnp.sqrt(total / panels_all + EPSILON)

    def pick(row, at):
        return jnp.sum(jnp.where(lane == at, row, 0.0), axis=1, keepdims=True)

    first_scale = scale_of(pick(jnp.sum(tops[...], axis=0), coeffs))

    lax.fori_loop(0, leaves // 4, add_far, 0)
    product = near_acc[...] * (first_scale * (1.0 / LIFT))
    unit = start_ref[...] * first_scale
    out_ref[0] = product
    along = total_of(unit * product)
    length = total_of(unit * unit)
    part = jnp.where(length > 0.0, along / length, 0.0)
    beyond = total_of((product - part * unit) ** 2)
    sums = jnp.where(
        lane == coeffs, along, jnp.where(lane == coeffs + 1, length, jnp.where(
            lane == coeffs + 2, beyond, part
        ))
    )
    pack(parcel2, tops2, area_ref[...] * product, sums)
    tops2_x[0]()
    parcel2_c[0]()
    tops2_x[1]()
    tops2_c[0]()
    parcel2_c[1]()
    unpack(parcel2)

    def near_second(l, c):
        acc = jnp.zeros((panels, LANES), jnp.float32)
        for n in range(entries - 1):
            index, scale = source_of(l, n)
            acc = spread(acc, kmat[l * entries + n], charge_rows(parcel2, index, scale))
        acc = spread(acc, kmat[l * entries + entries - 1], own_rows(parcel2, l))
        near_acc[pl.ds(l, 1), :] = to_row(acc)
        find_local(l)
        return c

    lax.fori_loop(0, leaves, near_second, 0)
    tops2_c[1]()
    find_down(tops2)
    rows = tops2[...].reshape(groups * devs, LANES)

    def column(at):
        return jnp.sum(jnp.where(lane == at, rows, 0.0), axis=1, keepdims=True)

    lengths = column(coeffs + 1)
    projection = total_of(column(coeffs)) / total_of(lengths)
    beyond = total_of(column(coeffs + 2) + (column(coeffs + 3) - projection) ** 2 * lengths)
    second_scale = scale_of(beyond)

    lax.fori_loop(0, leaves // 4, add_far, 0)
    out_ref[1] = (near_acc[...] - projection * out_ref[0]) * second_scale

    for copies in (
        points_c, parcel_c, parcel2_c, tops_c, tops2_c, tops_x, tops2_x
    ):
        copies[2]()


def per_device(
    start, coords, area, near_list, basis, far_leaf, couple_leaf, transfer, far_top, couple_top
):
    leaves, panels = start.shape
    entries = near_list.shape[1]
    coeffs = basis.shape[1]
    devs = lax.axis_size("dev")
    groups = lax.axis_size("group")
    smem = pl.BlockSpec(memory_space=pltpu.SMEM)
    anywhere = pl.BlockSpec(memory_space=pl.ANY)
    f32 = jnp.float32
    parcel_rows = panels // LANES * leaves + leaves // 2
    both = pl.pallas_call(
        functools.partial(kernel, devs, groups),
        out_shape=jax.ShapeDtypeStruct((2, leaves, panels), f32),
        in_specs=[smem] * 3 + [anywhere] * 7,
        out_specs=pl.BlockSpec(memory_space=pltpu.VMEM),
        scratch_shapes=[
            pltpu.VMEM(start.shape, f32),
            pltpu.VMEM(area.shape, f32),
            pltpu.VMEM(basis.shape, f32),
            pltpu.VMEM(couple_leaf.shape, f32),
            pltpu.VMEM(transfer.shape, f32),
            pltpu.VMEM(couple_top.shape, f32),
            pltpu.VMEM((devs, 3, leaves, panels), f32),
            pltpu.VMEM((devs, parcel_rows, LANES), f32),
            pltpu.VMEM((devs, parcel_rows, LANES), f32),
            pltpu.VMEM((groups * devs, 1, LANES), f32),
            pltpu.VMEM((groups * devs, 1, LANES), f32),
            pltpu.VMEM((leaves * entries, panels, panels), f32),
            pltpu.VMEM((leaves, panels), f32),
            pltpu.VMEM((leaves // 2, LANES), f32),
            pltpu.VMEM((devs, leaves, LANES), f32),
            pltpu.VMEM((leaves, coeffs, LANES), f32),
            pltpu.VMEM((leaves, panels, 48), jnp.bfloat16),
            pltpu.SemaphoreType.DMA((7,)),
            pltpu.SemaphoreType.DMA((5, devs)),
            pltpu.SemaphoreType.DMA((5, devs)),
            pltpu.SemaphoreType.DMA((2, groups)),
            pltpu.SemaphoreType.DMA((2, groups)),
        ],
        compiler_params=pltpu.CompilerParams(
            collective_id=0, has_side_effects=True, vmem_limit_bytes=60 * 1024 * 1024
        ),
    )(
        near_list.T, far_leaf.T, far_top, start, jnp.transpose(coords, (1, 0, 2)), area, basis,
        couple_leaf, transfer, couple_top,
    )
    return both[0], both[1]


def solution(mesh):
    rows = P(("group", "dev"), None)
    blocks = P(("group", "dev"), None, None)
    in_specs = (rows, blocks, rows, rows, blocks, rows, blocks, blocks, rows, blocks)
    return jax.shard_map(
        per_device, mesh=mesh, in_specs=in_specs, out_specs=(rows, rows), check_vma=False
    )
```

```python
import functools
import math

import jax
import jax.numpy as jnp
from jax import lax
from jax.experimental import pallas as pl
from jax.experimental.pallas import tpu as pltpu
from jax.sharding import PartitionSpec as P

FOUR_PI = 4.0 * math.pi
SOFTENING = 0.01
EPSILON = 1e-06
LIFT = 1024.0
MESH = pl.DeviceIdType.MESH
LANES = 128


def thirds(x):
    high = x.astype(jnp.bfloat16).astype(jnp.float32)
    rest = x - high
    middle = rest.astype(jnp.bfloat16).astype(jnp.float32)
    return high, middle, rest - middle


def kernel(
    devs, groups, near_ref, far_ref, top_ref, start_hbm, coords_hbm, area_hbm, basis_hbm,
    couple_hbm, transfer_hbm, ctop_hbm, out_ref, start_ref, area_ref, basis_ref, couple_ref,
    transfer_ref, ctop_ref, points, parcel, parcel2, tops, tops2, kmat, near_acc, down_ref,
    moms, locs, aims, kself, load_sem, send_sem, recv_sem, xsend_sem, xrecv_sem,
):
    leaves, panels = start_ref.shape
    entries = near_ref.shape[0]
    coeffs = basis_ref.shape[1]
    fars = far_ref.shape[0]
    pairs = leaves // 2
    halves = panels // LANES
    mom_row = halves * leaves
    me = lax.axis_index("dev")
    grp = lax.axis_index("group")

    def dev_peer(k):
        return (grp, lax.rem(me + k, devs))

    def grp_peer(k):
        return (lax.rem(grp + k, groups), me)

    barrier = pltpu.get_barrier_semaphore()

    def greet_dev(k, c):
        pl.semaphore_signal(barrier, inc=1, device_id=dev_peer(k), device_id_type=MESH)
        return c

    def greet_grp(k, c):
        pl.semaphore_signal(barrier, inc=1, device_id=grp_peer(k), device_id_type=MESH)
        return c

    lax.fori_loop(1, devs, greet_dev, 0)
    lax.fori_loop(1, groups, greet_grp, 0)

    loads = [
        pltpu.make_async_copy(source, target, load_sem.at[n])
        for n, (source, target) in enumerate((
            (start_hbm, start_ref), (area_hbm, area_ref), (basis_hbm, basis_ref),
            (transfer_hbm, transfer_ref), (coords_hbm, points.at[me]), (ctop_hbm, ctop_ref),
            (couple_hbm, couple_ref),
        ))
    ]
    for load in loads:
        load.start()

    def exchange(sems, count, mine, peer, source, block):
        send, recv = sems

        def copy(src, dst, k):
            return pltpu.make_async_remote_copy(
                src_ref=src, dst_ref=dst, send_sem=send(k), recv_sem=recv(k),
                device_id=peer(k), device_id_type=MESH,
            )

        def start(k, c):
            copy(source, block(mine), k).start()
            return c

        def arrive(k, c):
            landed = block(lax.rem(mine - k + count, count))
            copy(landed, landed, k).wait_recv()
            return c

        def sent(k, c):
            copy(source, block(mine), k).wait_send()
            return c

        return tuple(
            functools.partial(lax.fori_loop, 1, count, f, 0) for f in (start, arrive, sent)
        )

    def in_group(phase, source, block):
        sems = (lambda k: send_sem.at[phase, k], lambda k: recv_sem.at[phase, k])
        return exchange(sems, devs, me, dev_peer, source, block)

    def across(phase, buf):
        sems = (lambda k: xsend_sem.at[phase, k], lambda k: xrecv_sem.at[phase, k])
        return exchange(
            sems, groups, grp, grp_peer, buf.at[me * groups + grp],
            lambda g: buf.at[me * groups + g],
        )

    def line(buf):
        return lambda d: buf.at[pl.ds(d * groups, groups)]

    points_c = in_group(0, coords_hbm, lambda d: points.at[d])
    parcel_c = in_group(1, parcel.at[me], lambda d: parcel.at[d])
    parcel2_c = in_group(2, parcel2.at[me], lambda d: parcel2.at[d])
    tops_c = in_group(3, line(tops)(me), line(tops))
    tops2_c = in_group(4, line(tops2)(me), line(tops2))
    tops_x = across(0, tops)
    tops2_x = across(1, tops2)

    lane = lax.broadcasted_iota(jnp.int32, (1, LANES), 1)
    low_half = lane < coeffs
    row_r = lax.broadcasted_iota(jnp.int32, (coeffs, LANES), 0)
    lane_r = lax.broadcasted_iota(jnp.int32, (coeffs, LANES), 1)
    twice_eye = lax.rem(lane_r, coeffs) == row_r
    row_p = lax.broadcasted_iota(jnp.int32, (LANES, LANES), 0)
    lane_p = lax.broadcasted_iota(jnp.int32, (LANES, LANES), 1)
    eye = row_p == lane_p
    row8 = lax.broadcasted_iota(jnp.int32, (8, panels), 0)

    def lane_sum(x):
        total = x[:, :LANES]
        for j in range(1, x.shape[1] // LANES):
            total = total + x[:, j * LANES:(j + 1) * LANES]
        return jnp.sum(total, axis=1, keepdims=True)

    def total_of(x):
        return jnp.sum(jnp.sum(x, axis=0, keepdims=True), axis=1, keepdims=True)

    def twice_row(column):
        return jnp.sum(jnp.where(twice_eye, column, 0.0), axis=0, keepdims=True)

    def moment_row(index):
        return moms[index // leaves, pl.ds(lax.rem(index, leaves), 1), :]

    def pack(table, clusters, charges, sums):
        for h in range(halves):
            table[me, h * leaves:(h + 1) * leaves, :] = charges[:, h * LANES:(h + 1) * LANES]

        def body(i, c):
            rows = []
            for q in range(4):
                l = 4 * i + q
                total = jnp.zeros((coeffs, LANES), jnp.float32)
                for h in range(halves):
                    row = table[me, pl.ds(h * leaves + l, 1), :]
                    total = total + basis_ref[l, :, h * LANES:(h + 1) * LANES] * row
                rows.append(twice_row(lane_sum(total)))
            for q in range(4):
                moms[me, pl.ds(4 * i + q, 1), :] = rows[q]
            return c

        lax.fori_loop(0, leaves // 4, body, 0)
        table[me, mom_row:mom_row + pairs, :] = jnp.where(
            low_half, moms[me, :pairs, :], moms[me, pairs:, :]
        )
        total = jnp.zeros((coeffs, LANES), jnp.float32)
        for j in range(pairs):
            pair = jnp.where(
                low_half, moms[me, 2 * j:2 * j + 1, :], moms[me, 2 * j + 1:2 * j + 2, :]
            )
            total = total + transfer_ref[0, :, j * LANES:(j + 1) * LANES] * pair
        clusters[me * groups + grp] = jnp.where(low_half, twice_row(lane_sum(total)), sums)

    def unpack(table):
        def body(d, c):
            both = table[d, mom_row:mom_row + pairs, :]
            turned = pltpu.roll(both, coeffs, 1)
            moms[d, :pairs, :] = jnp.where(low_half, both, turned)
            moms[d, pairs:, :] = jnp.where(low_half, turned, both)
            return c

        lax.fori_loop(0, devs, body, 0)

    def cluster_row(clusters, index):
        return clusters[lax.rem(index, devs) * groups + index // devs]

    def find_down(clusters):
        total = jnp.zeros((coeffs, LANES), jnp.float32)
        for j in range(top_ref.shape[1] // 2):
            pair = jnp.where(
                low_half, cluster_row(clusters, top_ref[0, 2 * j]),
                pltpu.roll(cluster_row(clusters, top_ref[0, 2 * j + 1]), coeffs, 1),
            )
            total = total + ctop_ref[0, :, j * LANES:(j + 1) * LANES] * pair
        level = lane_sum(total)
        for j in range(pairs):
            down_ref[j:j + 1, :] = jnp.sum(
                transfer_ref[0, :, j * LANES:(j + 1) * LANES] * level, axis=0, keepdims=True
            )

    def find_local(l):
        total = jnp.zeros((coeffs, LANES), jnp.float32)
        for j in range(fars // 2):
            pair = jnp.where(
                low_half, moment_row(far_ref[2 * j, l]), moment_row(far_ref[2 * j + 1, l])
            )
            total = total + couple_ref[l, :, j * LANES:(j + 1) * LANES] * pair
        locs[l] = total

    def add_far(i, c):
        rows = []
        for q in range(4):
            l = 4 * i + q
            half = (q % 2) * coeffs
            down = down_ref[pl.ds(2 * i + q // 2, 1), :]
            total = locs[l] + jnp.where(lane_r == row_r + half, down, 0.0)
            rows.append(jnp.sum(basis_ref[l] * lane_sum(total), axis=0, keepdims=True))
        for q in range(4):
            at = pl.ds(4 * i + q, 1)
            near_acc[at, :] = near_acc[at, :] + rows[q]
        return c

    def source_of(l, n):
        own = (grp * devs + me) * leaves + l
        named = near_ref[n, l]
        named = jnp.where(named == own, near_ref[entries - 1, l], named)
        live = named >= 0
        index = jnp.where(live, named - grp * (devs * leaves), me * leaves + l)
        index = jnp.clip(index, 0, devs * leaves - 1)
        return index, jnp.where(live, 1.0 / FOUR_PI, 0.0)

    def point_rows(index):
        device, leaf = index // leaves, lax.rem(index, leaves)
        return [points[device, c, pl.ds(leaf, 1), :] for c in range(3)]

    def charge_rows(table, index, scale):
        device, leaf = index // leaves, lax.rem(index, leaves)
        return [
            table[device, pl.ds(h * leaves + leaf, 1), :] * scale for h in range(halves)
        ]

    def stack8(rows):
        total = jnp.zeros((8, panels), jnp.float32)
        for c, row in enumerate(rows):
            total = jnp.where(row8 == c, row, total)
        return total

    def to_row(acc):
        column = jnp.sum(acc, axis=1, keepdims=True)
        parts = [
            jnp.sum(
                jnp.where(eye, column[h * LANES:(h + 1) * LANES], 0.0), axis=0, keepdims=True
            )
            for h in range(panels // LANES)
        ]
        return jnp.concatenate(parts, axis=1)

    def sources_of(rows):
        x, y, z = rows
        high, middle, low = thirds(stack8((x, y, z, jnp.ones_like(x), x * x + y * y + z * z)))
        stacked = jnp.concatenate((high, middle, high, middle, low, high), axis=0)
        return stacked.astype(jnp.bfloat16)

    def coupling_of(targets, sources):
        return lax.rsqrt(jnp.dot(targets, sources, preferred_element_type=jnp.float32))

    loads[0].wait()
    loads[1].wait()
    squares = total_of(start_ref[...] * start_ref[...])
    pl.semaphore_wait(barrier, devs + groups - 2)
    points_c[0]()
    loads[2].wait()
    loads[3].wait()
    pack(parcel, tops, area_ref[...] * (start_ref[...] * LIFT), squares)
    parcel_c[0]()
    tops_x[0]()
    loads[4].wait()

    def near_self(l, c):
        rows = [points[me, axis, pl.ds(l, 1), :] for axis in range(3)]
        x, y, z = rows
        size = x * x + y * y + z * z + SOFTENING
        high, middle, low = thirds(
            stack8((-2.0 * x, -2.0 * y, -2.0 * z, size, jnp.ones_like(x)))
        )
        targets = jnp.concatenate((high, high, middle, middle, high, low), axis=0)
        targets = jnp.transpose(targets).astype(jnp.bfloat16)
        aims[l] = targets
        kself[l] = coupling_of(targets, sources_of(rows))
        return c

    lax.fori_loop(0, leaves, near_self, 0)
    tops_x[1]()
    tops_c[0]()
    loads[5].wait()
    loads[6].wait()
    points_c[1]()
    parcel_c[1]()
    unpack(parcel)

    def own_rows(table, l):
        return [
            table[me, pl.ds(h * leaves + l, 1), :] * (1.0 / FOUR_PI) for h in range(halves)
        ]

    def spread(acc, coupling, rows):
        for h, row in enumerate(rows):
            acc = acc + coupling[:, h * LANES:(h + 1) * LANES] * row
        return acc

    def near_first(i, c):
        rows = []
        for q in range(4):
            l = 4 * i + q
            acc = jnp.zeros((panels, LANES), jnp.float32)
            for n in range(entries - 1):
                index, scale = source_of(l, n)
                coupling = coupling_of(aims[l], sources_of(point_rows(index)))
                kmat[l * (entries - 1) + n] = coupling
                acc = spread(acc, coupling, charge_rows(parcel, index, scale))
            acc = spread(acc, kself[l], own_rows(parcel, l))
            rows.append(to_row(acc))
            find_local(l)
        for q in range(4):
            near_acc[pl.ds(4 * i + q, 1), :] = rows[q]
        return c

    lax.fori_loop(0, leaves // 4, near_first, 0)
    tops_c[1]()
    find_down(tops)

    panels_all = float(leaves * panels * devs * groups)

    def scale_of(total):
        return 1.0 / jnp.sqrt(total / panels_all + EPSILON)

    def pick(row, at):
        return jnp.sum(jnp.where(lane == at, row, 0.0), axis=1, keepdims=True)

    first_scale = scale_of(pick(jnp.sum(tops[...], axis=0), coeffs))

    lax.fori_loop(0, leaves // 4, add_far, 0)
    product = near_acc[...] * (first_scale * (1.0 / LIFT))
    unit = start_ref[...] * first_scale
    out_ref[0] = product
    along = total_of(unit * product)
    length = total_of(unit * unit)
    part = jnp.where(length > 0.0, along / length, 0.0)
    beyond = total_of((product - part * unit) ** 2)
    sums = jnp.where(
        lane == coeffs, along, jnp.where(lane == coeffs + 1, length, jnp.where(
            lane == coeffs + 2, beyond, part
        ))
    )
    pack(parcel2, tops2, area_ref[...] * product, sums)
    tops2_x[0]()
    parcel2_c[0]()
    tops2_x[1]()
    tops2_c[0]()
    parcel2_c[1]()
    unpack(parcel2)

    def near_second(i, c):
        rows = []
        for q in range(4):
            l = 4 * i + q
            acc = jnp.zeros((panels, LANES), jnp.float32)
            for n in range(entries - 1):
                index, scale = source_of(l, n)
                at = l * (entries - 1) + n
                acc = spread(acc, kmat[at], charge_rows(parcel2, index, scale))
            acc = spread(acc, kself[l], own_rows(parcel2, l))
            rows.append(to_row(acc))
            find_local(l)
        for q in range(4):
            near_acc[pl.ds(4 * i + q, 1), :] = rows[q]
        return c

    lax.fori_loop(0, leaves // 4, near_second, 0)
    tops2_c[1]()
    find_down(tops2)
    rows = tops2[...].reshape(groups * devs, LANES)

    def column(at):
        return jnp.sum(jnp.where(lane == at, rows, 0.0), axis=1, keepdims=True)

    lengths = column(coeffs + 1)
    projection = total_of(column(coeffs)) / total_of(lengths)
    beyond = total_of(column(coeffs + 2) + (column(coeffs + 3) - projection) ** 2 * lengths)
    second_scale = scale_of(beyond)

    lax.fori_loop(0, leaves // 4, add_far, 0)
    out_ref[1] = (near_acc[...] - projection * out_ref[0]) * second_scale

    for copies in (
        points_c, parcel_c, parcel2_c, tops_c, tops2_c, tops_x, tops2_x
    ):
        copies[2]()


def per_device(
    start, coords, area, near_list, basis, far_leaf, couple_leaf, transfer, far_top, couple_top
):
    leaves, panels = start.shape
    entries = near_list.shape[1]
    coeffs = basis.shape[1]
    devs = lax.axis_size("dev")
    groups = lax.axis_size("group")
    smem = pl.BlockSpec(memory_space=pltpu.SMEM)
    anywhere = pl.BlockSpec(memory_space=pl.ANY)
    f32 = jnp.float32
    parcel_rows = panels // LANES * leaves + leaves // 2
    both = pl.pallas_call(
        functools.partial(kernel, devs, groups),
        out_shape=jax.ShapeDtypeStruct((2, leaves, panels), f32),
        in_specs=[smem] * 3 + [anywhere] * 7,
        out_specs=pl.BlockSpec(memory_space=pltpu.VMEM),
        scratch_shapes=[
            pltpu.VMEM(start.shape, f32),
            pltpu.VMEM(area.shape, f32),
            pltpu.VMEM(basis.shape, f32),
            pltpu.VMEM(couple_leaf.shape, f32),
            pltpu.VMEM(transfer.shape, f32),
            pltpu.VMEM(couple_top.shape, f32),
            pltpu.VMEM((devs, 3, leaves, panels), f32),
            pltpu.VMEM((devs, parcel_rows, LANES), f32),
            pltpu.VMEM((devs, parcel_rows, LANES), f32),
            pltpu.VMEM((groups * devs, 1, LANES), f32),
            pltpu.VMEM((groups * devs, 1, LANES), f32),
            pltpu.VMEM((leaves * (entries - 1), panels, panels), f32),
            pltpu.VMEM((leaves, panels), f32),
            pltpu.VMEM((leaves // 2, LANES), f32),
            pltpu.VMEM((devs, leaves, LANES), f32),
            pltpu.VMEM((leaves, coeffs, LANES), f32),
            pltpu.VMEM((leaves, panels, 48), jnp.bfloat16),
            pltpu.VMEM((leaves, panels, panels), f32),
            pltpu.SemaphoreType.DMA((7,)),
            pltpu.SemaphoreType.DMA((5, devs)),
            pltpu.SemaphoreType.DMA((5, devs)),
            pltpu.SemaphoreType.DMA((2, groups)),
            pltpu.SemaphoreType.DMA((2, groups)),
        ],
        compiler_params=pltpu.CompilerParams(
            collective_id=0, has_side_effects=True, vmem_limit_bytes=60 * 1024 * 1024
        ),
    )(
        near_list.T, far_leaf.T, far_top, start, jnp.transpose(coords, (1, 0, 2)), area, basis,
        couple_leaf, transfer, couple_top,
    )
    return both[0], both[1]


def solution(mesh):
    rows = P(("group", "dev"), None)
    blocks = P(("group", "dev"), None, None)
    in_specs = (rows, blocks, rows, rows, blocks, rows, blocks, blocks, rows, blocks)
    return jax.shard_map(
        per_device, mesh=mesh, in_specs=in_specs, out_specs=(rows, rows), check_vma=False
    )
```
